32 devices in a mesh: section: 2 (over x), dp: 16 (over z, y, core).
Axes of the slice: x: 2, y: 2, z: 4, core: 2. Of those that a mesh axis runs over, the one named last changes fastest.
Arguments:
- stream_in: bfloat16 [128, 8192], P(None, 'dp'), may hold values from -6 to 6
- gains: float32 [2, 8192], P('section'), may hold values from 0.5 to 1.5
- weights: bfloat16 [2, 8192, 8192], P('section', 'dp'), may hold values from -6 to 6
- masks: int32 [2, 8192, 128], P('section', 'dp'), may hold values 0 or 1
- inv_hessian: float32 [2, 64, 128, 128], P('section', 'dp'), may hold values from -0.025 to 3.2
Outputs:
- stream_out: bfloat16 [2, 128, 8192], P('section', None, 'dp')
- refitted: bfloat16 [2, 8192, 8192], P('section', 'dp')
The draws below stay inside these ranges and needn't reach their ends.
All inputs are finite; a program needn't handle non-finite values. No bound on the sum of `masks` on one device may be relied on, other than what follows from the above.
Results may differ from the reference program's by a relative error of at most 0.015.
Values may be sent and summed in bfloat16 or wider, within the bound.
A program may use at most 128 MiB of HBM per device.

```python
import jax
import jax.numpy as jnp
from jax import lax

D = 8192
BLOCK = 128
TOKENS = 128
SECTIONS = 2
NB = 64
N_SECTION = 2


def draw_inv_hessian(key, part):
    first, second = jax.random.split(jax.random.fold_in(key, 17))
    diagonal = jax.random.uniform(first, (SECTIONS, NB, BLOCK), jnp.float32, 1.6, 3.2)
    spread = jax.random.uniform(second, (SECTIONS, NB, BLOCK, BLOCK), jnp.float32, -0.025, 0.025)
    symmetric = 0.5 * (spread + jnp.swapaxes(spread, 2, 3))
    identity = jnp.eye(BLOCK, dtype=jnp.float32)
    return symmetric * (1.0 - identity) + diagonal[..., None] * identity


def with_ends(drawn, key, low, top_value):
    place = [jax.random.randint(jax.random.fold_in(key, axis), (), 0, length) for axis, length in enumerate(drawn.shape)]
    longest = drawn.shape.index(max(drawn.shape))
    neighbour = place[:longest] + [(place[longest] + 1) % drawn.shape[longest]] + place[longest + 1:]
    return drawn.at[tuple(place)].set(low).at[tuple(neighbour)].set(top_value)


def steps_of(own_key, extent, pieces, low, largest):
    def one(position, blocks):
        heights = jax.random.uniform(jax.random.fold_in(jax.random.fold_in(own_key, 6), position), (blocks,), jnp.float32, low / len(pieces), largest / len(pieces))
        return jnp.repeat(jnp.exp(heights), extent[position] // blocks).reshape((-1,) + (1,) * (len(extent) - position - 1))

    level = one(*pieces[0])
    for cut in pieces[1:]:
        level = level * one(*cut)
    return level


def gaussian(key, shape, scale, limit, shards=(), kind=jnp.bfloat16):
    values = scale * jax.random.normal(key, shape, jnp.float32)
    if shards:
        values = values * steps_of(key, shape, shards, -0.22, 0.18)
    return jnp.clip(values, -limit, limit).astype(kind)


def setup_inputs(seed: int = 0) -> dict:
    seeds = jax.random.split(jax.random.key(seed), 6)
    stream_in = gaussian(seeds[0], (TOKENS, D), 1.0, 6.0, ((1, 16),))
    gains = jnp.clip(1.0 + 0.1 * jax.random.normal(seeds[1], (SECTIONS, D), jnp.float32), 0.5, 1.5)
    weights = gaussian(seeds[2], (SECTIONS, D, D), 1.0, 6.0, ((0, 2), (1, 16)))
    masks = with_ends((jax.random.randint(seeds[3], (SECTIONS, D, 2 * NB), 0, 2) < 1).astype(jnp.int32), jax.random.fold_in(seeds[3], 1), 0, 1)
    inv_hessian = draw_inv_hessian(jax.random.fold_in(seeds[5], 71), 0)
    return dict(stream_in=stream_in, gains=gains, weights=weights, masks=masks, inv_hessian=inv_hessian)


def reference(stream_in, gains, weights, masks, inv_hessian):
    stream = stream_in
    outputs = []
    refits = []
    for layer in range(N_SECTION):
        widened = stream.astype(jnp.float32)
        mean_square = lax.optimization_barrier(jnp.mean(widened * widened, axis=1, keepdims=True))
        normed = (widened * lax.rsqrt(mean_square + 1e-05) * gains[layer]).astype(jnp.bfloat16)
        keep = jnp.repeat(masks[layer], BLOCK // 2, axis=1)
        kept_rows = weights[layer] * keep.astype(jnp.bfloat16)
        projected = jnp.dot(normed, kept_rows.T, preferred_element_type=jnp.float32) * D ** (-0.5)
        stream = (widened + projected).astype(jnp.bfloat16)
        outputs.append(stream)
        blocks = normed.astype(jnp.float32).reshape(TOKENS, NB, BLOCK)
        gram_block = jnp.einsum('tbi,tbj->bij', blocks, blocks, precision=lax.Precision.HIGHEST)
        hessian = gram_block * (1.0 / TOKENS)
        removed = weights[layer].astype(jnp.float32) * (1 - keep).astype(jnp.float32)
        removed = removed.reshape(D, NB, BLOCK)
        gradient = jnp.einsum('rbi,bij->rbj', removed, hessian, precision=lax.Precision.HIGHEST)
        update_step = jnp.einsum('rbi,bij->rbj', gradient, inv_hessian[layer], precision=lax.Precision.HIGHEST)
        refitted = keep.astype(jnp.float32) * (weights[layer].astype(jnp.float32) + update_step.reshape(D, D))
        refits.append(refitted.astype(jnp.bfloat16))
    return (jnp.stack(outputs), jnp.stack(refits))
```

```python
import functools

import jax
import jax.numpy as jnp
from jax import lax
from jax.experimental import pallas as pl
from jax.experimental.pallas import tpu as pltpu
from jax.sharding import PartitionSpec as P

BLOCK = 128
HALF = BLOCK // 2
VMEM_BYTES = 32 * 1024 * 1024


def keep_columns(masks_ref, cols):
    entries = masks_ref[0].astype(jnp.float32).astype(jnp.bfloat16)
    first = lax.broadcasted_iota(jnp.int32, (entries.shape[1], cols), 0) * HALF
    column = lax.broadcasted_iota(jnp.int32, (entries.shape[1], cols), 1) + pl.program_id(0) * cols
    spread = ((column >= first) & (column < first + HALF)).astype(jnp.float32).astype(jnp.bfloat16)
    return jnp.dot(entries, spread, preferred_element_type=jnp.float32)


def project_kernel(last, width, tokens, *refs):
    x_ref, gain_ref, weights_ref, masks_ref, window_ref, own_gain_ref, inverse_ref = refs[:7]
    out_ref = refs[7]
    total, squares = refs[-2:]
    step = pl.program_id(0)

    @pl.when(step == 0)
    def _():
        total[...] = jnp.zeros_like(total)
        squares[...] = jnp.zeros_like(squares)

    x = x_ref[0].astype(jnp.float32)
    squares[...] += jnp.sum(x * x, axis=1, keepdims=True)
    scaled = (x * gain_ref[...]).astype(jnp.bfloat16)
    kept = weights_ref[0] * keep_columns(masks_ref, x.shape[1]).astype(jnp.bfloat16)
    total[...] += lax.dot_general(
        scaled, kept, (((1,), (1,)), ((), ())), preferred_element_type=jnp.float32
    )

    @pl.when(step == pl.num_programs(0) - 1)
    def _():
        inverse_rms = lax.rsqrt(squares[...] * (1.0 / width) + 1e-05)
        window = window_ref[...].astype(jnp.float32)
        out_ref[...] = (window + total[...] * inverse_rms * width ** (-0.5)).astype(jnp.bfloat16)
        if last:
            factor_ref = refs[8]
            normed = (window * inverse_rms * own_gain_ref[...]).astype(jnp.bfloat16)
            for block in range(normed.shape[1] // BLOCK):
                columns = normed[:, block * BLOCK : (block + 1) * BLOCK]
                hessian = lax.dot_general(
                    columns, columns, (((0,), (0,)), ((), ())), preferred_element_type=jnp.float32
                ) * (1.0 / tokens)
                factor_ref[block] = jnp.dot(
                    hessian,
                    inverse_ref[0, block],
                    precision=lax.Precision.HIGHEST,
                    preferred_element_type=jnp.float32,
                ).astype(jnp.bfloat16)


def project(gathered, gains, weights, masks, window, own_gain, inv_hessian, last):
    steps, tokens, cols = gathered.shape
    _, rows, width = weights.shape
    whole = lambda shape: pl.BlockSpec(shape, lambda c: (0,) * len(shape))
    out_shape = [jax.ShapeDtypeStruct(window.shape, jnp.bfloat16)]
    if last:
        out_shape.append(jax.ShapeDtypeStruct(inv_hessian.shape[1:], jnp.bfloat16))
    return pl.pallas_call(
        functools.partial(project_kernel, last, width, tokens),
        grid=(steps,),
        in_specs=[
            pl.BlockSpec((1, tokens, cols), lambda c: (c, 0, 0)),
            pl.BlockSpec((1, cols), lambda c: (0, c)),
            pl.BlockSpec((1, rows, cols), lambda c: (0, 0, c)),
            whole(masks.shape),
            whole(window.shape),
            whole(own_gain.shape),
            whole(inv_hessian.shape),
        ],
        out_specs=[whole(s.shape) for s in out_shape],
        out_shape=out_shape,
        scratch_shapes=[
            pltpu.VMEM((tokens, rows), jnp.float32),
            pltpu.VMEM((tokens, 1), jnp.float32),
        ],
        compiler_params=pltpu.CompilerParams(vmem_limit_bytes=VMEM_BYTES),
        cost_estimate=pl.CostEstimate(
            flops=2 * tokens * rows * width, bytes_accessed=2 * rows * width, transcendentals=0
        ),
    )(gathered, gains, weights, masks, window, own_gain, inv_hessian)


def refit_kernel(weights_ref, masks_ref, factor_ref, out_ref):
    cols = weights_ref.shape[2]
    keep = keep_columns(masks_ref, cols)
    weights = weights_ref[0].astype(jnp.float32)
    removed = (weights * (1.0 - keep)).astype(jnp.bfloat16)
    for block in range(cols // BLOCK):
        part = slice(block * BLOCK, (block + 1) * BLOCK)
        update = jnp.dot(removed[:, part], factor_ref[0, block], preferred_element_type=jnp.float32)
        out_ref[0, :, part] = (keep[:, part] * (weights[:, part] + update)).astype(jnp.bfloat16)


def refit(weights, masks, factors):
    steps, blocks = factors.shape[:2]
    _, rows, width = weights.shape
    cols = blocks * BLOCK
    return pl.pallas_call(
        refit_kernel,
        grid=(steps,),
        in_specs=[
            pl.BlockSpec((1, rows, cols), lambda c: (0, 0, c)),
            pl.BlockSpec(masks.shape, lambda c: (0, 0, 0)),
            pl.BlockSpec((1, blocks, BLOCK, BLOCK), lambda c: (c, 0, 0, 0)),
        ],
        out_specs=pl.BlockSpec((1, rows, cols), lambda c: (0, 0, c)),
        out_shape=jax.ShapeDtypeStruct(weights.shape, jnp.bfloat16),
        compiler_params=pltpu.CompilerParams(vmem_limit_bytes=VMEM_BYTES),
        cost_estimate=pl.CostEstimate(
            flops=2 * rows * width * BLOCK, bytes_accessed=4 * rows * width, transcendentals=0
        ),
    )(weights, masks, factors)


def body(stream_in, gains, weights, masks, inv_hessian):
    section_index = lax.axis_index("section")
    sections = lax.axis_size("section")
    owned_cols = stream_in.shape[1]
    own_gain = lax.dynamic_slice_in_dim(gains, lax.axis_index("dp") * owned_cols, owned_cols, 1)
    window = stream_in
    for moment in range(sections):
        last = moment == sections - 1
        gathered = lax.all_gather(window, "dp")
        results = project(gathered, gains, weights, masks, window, own_gain, inv_hessian, last)
        if not last:
            received = lax.ppermute(
                results[0], "section", [(source, source + 1) for source in range(sections - 1)]
            )
            window = jnp.where(section_index == 0, stream_in, received)
    stream_out, factor = results
    refitted = refit(weights, masks, lax.all_gather(factor, "dp"))
    return stream_out[None], refitted


def solution(mesh):
    placed = (
        P(None, "dp"),
        P("section", None),
        P("section", "dp", None),
        P("section", "dp", None),
        P("section", "dp", None, None),
    )
    return jax.shard_map(
        body,
        mesh=mesh,
        in_specs=placed,
        out_specs=(P("section", None, "dp"), P("section", "dp", None)),
        check_vma=False,
    )
```
